256 devices in a mesh: segment: 2 (over y_hi), shard: 64 (over x, y_lo, z), chan: 2 (over core).
Axes of the slice: x: 4, y: 4 (y_hi: 2, y_lo: 2; y = y_hi * 2 + y_lo), z: 8, core: 2. Of those that a mesh axis runs over, the one named last changes fastest.
Arguments:
- echoes: bfloat16 [2, 8192, 16384], P(None, ('chan', 'segment', 'shard')), parts along dimension 1, may hold values from -6 to 6
- replica: float32 [2, 2048], replicated, may hold values from -0.09375 to 0.09375
- rcmc_weights: float32 [8, 4096], replicated, may hold values from -2 to 2
- az_filter: bfloat16 [2, 4096, 16384], P(None, None, ('segment', 'shard')), may hold values from -4.1875 to 4.1875
Outputs:
- image: float32 [2, 8192, 16384], P(None, 'chan', ('segment', 'shard')), parts along dimension 1
The draws below stay inside these ranges and needn't reach their ends.
There are 2 independent parts, one for each index of `chan`. The reference program is written for one: setup_inputs(seed, part) draws one part's arguments, and reference() takes and returns one part's arrays. A program takes and returns all parts, laid end to end along the dimension named above; an argument that names none is the same for every part. Nothing has to cross between parts.
All inputs are finite; a program needn't handle non-finite values.
Results may differ from the reference program's by a relative error of at most 0.0003.
Values sent between devices are 32-bit elements; how exact they have to be, the bound alone decides.
A program may use at most 128 MiB of HBM per device.

```python
import math
import jax
import jax.numpy as jnp
from jax import lax

NR = 16384
PULSES = 4096
CHIRP = 2048
TAPS = 8


def levels(rng, shape, shards, least, high):
    level = 1.0
    for axis_at, shards_of in shards:
        steps = jax.random.uniform(jax.random.fold_in(jax.random.fold_in(rng, 6), axis_at), (shards_of,), jnp.float32, least / len(shards), high / len(shards))
        level = level * jnp.repeat(jnp.exp(steps), shape[axis_at] // shards_of).reshape((-1,) + (1,) * (len(shape) - 1 - axis_at))
    return level


def noise(stream_key, extent, deviation, most, shards=(), held_as=jnp.bfloat16):
    entries = jax.random.normal(stream_key, extent, jnp.float32) * deviation
    if len(shards) > 0:
        entries = levels(stream_key, extent, shards, -0.22, 0.18) * entries
    return jnp.clip(entries, min=-most, max=most).astype(held_as)


def setup_inputs(seed: int = 0, part: int = 0) -> dict:
    key_of = jax.random.split(jax.random.key(seed), 5)
    part_keys = jax.random.split(jax.random.fold_in(key_of[4], part), 5)
    return {
        "echoes": noise(part_keys[0], (2, PULSES, NR), 1.0, 6.0, ((1, 128),)),
        "replica": noise(key_of[1], (2, CHIRP), (2 * CHIRP) ** -0.5, 0.09375, (), jnp.float32),
        "rcmc_weights": noise(key_of[2], (TAPS, PULSES), TAPS ** -0.5, 2.0, (), jnp.float32),
        "az_filter": noise(key_of[3], (2, PULSES, NR), 0.7, 4.1875, ((2, 128),)),
    }


def reference(echoes, replica, rcmc_weights, az_filter):
    half_taps = TAPS // 2
    pulse_block = math.gcd(PULSES, 256)
    block_count = PULSES // pulse_block
    kernel_real = jnp.pad(replica[0], (0, NR - CHIRP))
    kernel_imag = jnp.pad(replica[1], (0, NR - CHIRP))
    kernel_conj = jnp.conj(jnp.fft.fft(lax.complex(kernel_real, kernel_imag)))

    def range_block(number):
        start = (number * pulse_block).astype(jnp.int32)
        echo_real = lax.dynamic_slice_in_dim(echoes[0], start, pulse_block, 0).astype(jnp.float32)
        echo_imag = lax.dynamic_slice_in_dim(echoes[1], start, pulse_block, 0).astype(jnp.float32)
        spectrum = jnp.fft.fft(lax.complex(echo_real, echo_imag), axis=1)
        return jnp.fft.ifft(spectrum * kernel_conj[None, :], axis=1)

    compressed = lax.map(range_block, jnp.arange(block_count, dtype=jnp.int32)).reshape(PULSES, NR)
    doppler = jnp.fft.fft(compressed, axis=0)
    padded = jnp.pad(doppler, ((0, 0), (half_taps, half_taps)))
    response = lax.complex(az_filter[0].astype(jnp.float32), az_filter[1].astype(jnp.float32))
    span_bins = math.gcd(NR, 1024)
    span_count = NR // span_bins

    def range_span(number):
        start = (number * span_bins).astype(jnp.int32)
        window = lax.dynamic_slice_in_dim(padded, start, span_bins + 2 * half_taps, 1)
        moved = rcmc_weights[0][:, None] * window[:, 0:span_bins]
        for offset in range(1, TAPS):
            moved = moved + rcmc_weights[offset][:, None] * window[:, offset:offset + span_bins]
        local_response = lax.dynamic_slice_in_dim(response, start, span_bins, 1)
        return jnp.fft.ifft(moved * local_response, axis=0)

    pieces = lax.map(range_span, jnp.arange(span_count, dtype=jnp.int32))
    focused = jnp.transpose(pieces, (1, 0, 2)).reshape(PULSES, NR)
    return jnp.stack([jnp.real(focused), jnp.imag(focused)]).astype(jnp.float32)
```

```python
import functools
import math

import jax
import jax.numpy as jnp
import ml_dtypes
import numpy as np
from jax import lax
from jax.experimental import pallas as pl
from jax.experimental.pallas import tpu as pltpu
from jax.sharding import PartitionSpec as P

MESH = pl.DeviceIdType.MESH
F32 = jnp.float32
BF16 = jnp.bfloat16
TAPS = 8
HALF = TAPS // 2
N = 128
J = 32
CHUNKS = ((0, 4), (4, 8), (12, 8), (20, 12))


def constant_tables():
    k = np.arange(N)
    ang = 2.0 * np.pi * ((k[:, None] * k[None, :]) % N) / N
    c, s = np.cos(ang), -np.sin(ang)
    left = np.block([[c, -s], [s, c]]).astype(np.float32)
    mats = []
    for m in (left, left.T):
        hi = m.astype(ml_dtypes.bfloat16)
        lo = (m - hi.astype(np.float32)).astype(ml_dtypes.bfloat16)
        mats += [hi, lo]
    mats = np.stack(mats)
    ang = 2.0 * np.pi * (k[:, None] * k[None, :]) / (N * N)
    twist = np.stack([np.cos(ang), -np.sin(ang)]).astype(np.float32)
    j = np.arange(J)
    ang = 2.0 * np.pi * (j[:, None] * k[None, :]) / (N * J)
    az = np.stack([np.cos(ang), -np.sin(ang)], axis=1).astype(np.float32)
    az = np.ascontiguousarray(np.broadcast_to(az[..., None], (J, 2, N, N)))
    return mats, twist, az


def split(v):
    hi = v.astype(BF16)
    return hi, (v - hi.astype(F32)).astype(BF16)


def dot(a, b):
    return jnp.dot(a, b, preferred_element_type=F32)


def left_mul(hi, lo, data):
    d_hi, d_lo = split(data)
    return dot(hi, d_hi) + dot(lo, d_hi) + dot(hi, d_lo)


def right_mul(data, hi, lo):
    d_hi, d_lo = split(data)
    return dot(d_hi, hi) + dot(d_lo, hi) + dot(d_hi, lo)


def add(a, b):
    return (a[0] + b[0], a[1] + b[1])


def sub(a, b):
    return (a[0] - b[0], a[1] - b[1])


def turn(a, angle_num, angle_den, sign):
    q = (8 * angle_num) % (8 * angle_den)
    if q == 0:
        return a
    if q == 2 * angle_den:
        return (-a[1], a[0]) if sign > 0 else (a[1], -a[0])
    if q == 4 * angle_den:
        return (-a[0], -a[1])
    if q == 6 * angle_den:
        return (a[1], -a[0]) if sign > 0 else (-a[1], a[0])
    ang = sign * 2.0 * math.pi * angle_num / angle_den
    c, s = math.cos(ang), math.sin(ang)
    return (a[0] * c - a[1] * s, a[0] * s + a[1] * c)


def fft(xs, sign):
    n = len(xs)
    if n == 1:
        return xs
    even, odd = fft(xs[0::2], sign), fft(xs[1::2], sign)
    out = [None] * n
    for k in range(n // 2):
        t = turn(odd[k], k, n, sign)
        out[k] = add(even[k], t)
        out[k + n // 2] = sub(even[k], t)
    return out


def fft32(xs, sign):
    cols = []
    for low in range(4):
        col = fft([xs[4 * high + low] for high in range(8)], sign)
        cols.append([turn(col[k], low * k, 32, sign) for k in range(8)])
    out = [None] * 32
    for k in range(8):
        four = fft([cols[low][k] for low in range(4)], sign)
        for k0 in range(4):
            out[k + 8 * k0] = four[k0]
    return out


def body(
    echoes, replica, weights, az_filter, mats_h, twist_h, aztw_h, out,
    e_v, u_v, rep_v, x_v, kern_v, s_v, r_v, y_v, w_t, w_b, azf_v, az_v, mats, twist, aztw,
    p_r, p_l, h_l, h_r, o_v, in_sem, send_sem, recv_sem, own_sem, halo_send, halo_recv, out_sem,
):
    seg, sh = lax.axis_index("segment"), lax.axis_index("shard")
    x, y, z = sh // 16, seg * 2 + (sh // 8) % 2, sh % 8
    me = seg * 64 + sh

    def peer(i):
        px, py, pz = (x + i // 32) % 4, (y + (i // 8) % 4) % 4, (z + i % 8) % 8
        s, h = py // 2, (px * 2 + py % 2) * 8 + pz
        return s, h, s * 64 + h

    loads = [
        pltpu.make_async_copy(replica, rep_v, in_sem.at[0]),
        pltpu.make_async_copy(mats_h, mats, in_sem.at[1]),
        pltpu.make_async_copy(twist_h, twist, in_sem.at[2]),
        pltpu.make_async_copy(echoes.at[:, pl.ds(0, 16)], e_v.at[:, pl.ds(0, 16)], in_sem.at[3]),
        pltpu.make_async_copy(echoes.at[:, pl.ds(16, 16)], e_v.at[:, pl.ds(16, 16)], in_sem.at[4]),
        pltpu.make_async_copy(weights, w_t, in_sem.at[5]),
        pltpu.make_async_copy(az_filter, az_v, in_sem.at[6]),
        pltpu.make_async_copy(aztw_h, aztw, in_sem.at[7]),
    ]
    for load in loads:
        load.start()
    barrier = pltpu.get_barrier_semaphore()

    def greet(i, c):
        s, h, _ = peer(i)
        pl.semaphore_signal(
            barrier, inc=1, device_id={"segment": s, "shard": h}, device_id_type=MESH
        )
        return c

    lax.fori_loop(1, N, greet, 0)

    for i in range(3):
        loads[i].wait()
    x_v[...] = jnp.zeros_like(x_v)
    for a in range(16):
        x_v[pl.ds(a, 1), :] = rep_v[0:1, 128 * a : 128 * a + 128]
        x_v[pl.ds(128 + a, 1), :] = rep_v[1:2, 128 * a : 128 * a + 128]
    t_re, t_im = twist[0], twist[1]
    mid = left_mul(mats[0], mats[1], x_v[...])
    m_re, m_im = mid[:N], mid[N:]
    mid = jnp.concatenate([m_re * t_re - m_im * t_im, m_re * t_im + m_im * t_re], axis=1)
    spec = right_mul(mid, mats[2], mats[3]) * (1.0 / (N * N))
    kern_v[0] = spec[:, :N]
    kern_v[1] = spec[:, N:]

    def unpack(half):
        def one(a, c):
            cols = pl.ds(pl.multiple_of(a * 128, 128), 128)
            rows = pl.ds(pl.multiple_of(a * 16, 16), 16)
            for part in range(2):
                u_v[part, rows, :] = e_v[part, pl.ds(16 * half, 16), cols].astype(F32)
            return c

        lax.fori_loop(0, N, one, 0, unroll=8)

    def compress(pair, c):
        p = (2 * pair) % 16
        data = jnp.concatenate(
            [
                jnp.concatenate(
                    [u_v[part, pl.ds(p + i, N, stride=16), :] for part in range(2)], axis=0
                )
                for i in range(2)
            ],
            axis=1,
        ).astype(BF16)
        mid = dot(mats[0], data) + dot(mats[1], data)
        rows = []
        for i in range(2):
            m_re, m_im = mid[:N, i * N : i * N + N], mid[N:, i * N : i * N + N]
            rows.append(
                jnp.concatenate(
                    [m_re * twist[0] - m_im * twist[1], m_re * twist[1] + m_im * twist[0]], axis=1
                )
            )
        spec = right_mul(jnp.concatenate(rows, axis=0), mats[2], mats[3])
        rows = []
        for i in range(2):
            s_re, s_im = spec[i * N : i * N + N, :N], spec[i * N : i * N + N, N:]
            rows.append(
                jnp.concatenate(
                    [s_re * kern_v[0] + s_im * kern_v[1], s_im * kern_v[0] - s_re * kern_v[1]],
                    axis=1,
                )
            )
        mid = right_mul(jnp.concatenate(rows, axis=0), mats[0], mats[1])
        cols = []
        for i in range(2):
            m_re, m_im = mid[i * N : i * N + N, :N], mid[i * N : i * N + N, N:]
            cols.append(
                jnp.concatenate(
                    [m_re * twist[0] + m_im * twist[1], m_im * twist[0] - m_re * twist[1]], axis=0
                )
            )
        done = left_mul(mats[2], mats[3], jnp.concatenate(cols, axis=1))
        for i in range(2):
            for part in range(2):
                s_v[2 * pair + i, part] = done[part * N : part * N + N, i * N : i * N + N]
        return c

    def send(n):
        first, count = CHUNKS[n]
        rows = pl.ds(first, count)
        pltpu.make_async_copy(s_v.at[rows, :, me], r_v.at[rows, :, me], own_sem.at[n]).start()

        def one(i, c):
            s, h, at = peer(i)
            pltpu.make_async_remote_copy(
                src_ref=s_v.at[rows, :, at],
                dst_ref=r_v.at[rows, :, me],
                send_sem=send_sem.at[n],
                recv_sem=recv_sem.at[n],
                device_id={"segment": s, "shard": h},
                device_id_type=MESH,
            ).start()
            return c

        lax.fori_loop(1, N, one, 0)

    loads[3].wait()
    unpack(0)
    half = 0
    for n, (first, count) in enumerate(CHUNKS):
        start = first
        if first < 16 < first + count:
            lax.fori_loop(first // 2, 8, compress, 0)
            start = 16
        if start >= 16 and half == 0:
            half = 1
            loads[4].wait()
            unpack(1)
        lax.fori_loop(start // 2, (first + count) // 2, compress, 0)
        if n == 0:
            pl.semaphore_wait(barrier, N - 1)
        send(n)

    loads[5].wait()

    def spread(g, c):
        cols = pl.ds(pl.multiple_of(g * 128, 128), 128)
        across = jnp.transpose(w_t[:, cols])
        for t in range(TAPS):
            w_b[t, cols, :] = jnp.broadcast_to(across[:, t : t + 1], (N, N))
        return c

    lax.fori_loop(0, J, spread, 0)
    loads[6].wait()

    def widen(g, c):
        rows = pl.ds(pl.multiple_of(g * 128, 128), 128)
        for part in range(2):
            azf_v[part, rows, :] = az_v[part, rows, :].astype(F32)
        return c

    lax.fori_loop(0, J, widen, 0)
    loads[7].wait()

    def over_devices(pair, c):
        data = jnp.concatenate(
            [
                jnp.concatenate([r_v[2 * pair + i, 0], r_v[2 * pair + i, 1]], axis=0)
                for i in range(2)
            ],
            axis=1,
        )
        mid = left_mul(mats[0], mats[1], data)
        for i in range(2):
            m_re, m_im = mid[:N, i * N : i * N + N], mid[N:, i * N : i * N + N]
            a_re, a_im = aztw[2 * pair + i, 0], aztw[2 * pair + i, 1]
            y_v[2 * pair + i, 0] = m_re * a_re - m_im * a_im
            y_v[2 * pair + i, 1] = m_re * a_im + m_im * a_re
        return c

    for n, (first, count) in enumerate(CHUNKS):
        rows = pl.ds(first, count)
        pltpu.make_async_copy(s_v.at[rows, :, me], r_v.at[rows, :, me], own_sem.at[n]).wait()
        landed = r_v.at[rows, :, pl.ds(0, N - 1)]
        pltpu.make_async_copy(landed, landed, recv_sem.at[n]).wait()
        lax.fori_loop(first // 2, (first + count) // 2, over_devices, 0)

    lane = lax.broadcasted_iota(jnp.int32, (8, N), 1)
    slot = lane % 8

    def over_pulses(blk, c):
        rows = pl.ds(pl.multiple_of(blk * 8, 8), 8)
        vals = fft32([(y_v[j, 0, rows, :], y_v[j, 1, rows, :]) for j in range(J)], -1)
        for f2 in range(J):
            y_v[f2, 0, rows, :] = vals[f2][0]
            y_v[f2, 1, rows, :] = vals[f2][1]
        for grp in range(2):
            packed = []
            for part in range(2):
                acc = jnp.zeros((8, N), F32)
                for g in range(16):
                    moved = pltpu.roll(vals[16 * grp + g][part], (8 * g + 4) % N, 1)
                    acc = jnp.where(lane // 8 == g, moved, acc)
                packed.append(acc)
            p_r[blk, grp] = jnp.where(slot < 4, packed[0], pltpu.roll(packed[1], 4, 1))
            p_l[blk, grp] = jnp.where(slot < 4, pltpu.roll(packed[0], N - 4, 1), packed[1])
        return c

    lax.fori_loop(0, 16, over_pulses, 0)
    after, before = (me + 1) % N, (me + N - 1) % N
    right = {"segment": after // 64, "shard": after % 64}
    left = {"segment": before // 64, "shard": before % 64}
    to_right = pltpu.make_async_remote_copy(
        src_ref=p_r, dst_ref=h_l, send_sem=halo_send.at[0], recv_sem=halo_recv.at[0],
        device_id=right, device_id_type=MESH,
    )
    to_left = pltpu.make_async_remote_copy(
        src_ref=p_l, dst_ref=h_r, send_sem=halo_send.at[1], recv_sem=halo_recv.at[1],
        device_id=left, device_id_type=MESH,
    )
    to_right.start()
    to_left.start()
    to_right.wait()
    to_left.wait()

    has_left = jnp.where(me == 0, 0.0, 1.0)
    has_right = jnp.where(me == N - 1, 0.0, 1.0)

    def focus(blk, c):
        rows = pl.ds(pl.multiple_of(blk * 8, 8), 8)
        halos = []
        for grp in range(2):
            lft = h_l[blk, grp] * has_left
            rgt = h_r[blk, grp] * has_right
            halos.append(
                (
                    jnp.where(slot < 4, lft, pltpu.roll(rgt, 4, 1)),
                    jnp.where(slot < 4, pltpu.roll(lft, N - 4, 1), rgt),
                )
            )
        vals = []
        for f2 in range(J):
            frows = pl.ds(pl.multiple_of(f2 * 128 + blk * 8, 8), 8)
            taps = [w_b[t, frows, :] for t in range(TAPS)]
            moved = []
            for part in range(2):
                own = y_v[f2, part, rows, :]
                edge = pltpu.roll(halos[f2 // 16][part], (N - 8 * (f2 % 16) - 4) % N, 1)
                acc = taps[HALF] * own
                for t in range(TAPS):
                    if t != HALF:
                        wrapped = lane < t - HALF if t > HALF else lane >= N - HALF + t
                        src = jnp.where(wrapped, edge, own)
                        acc = acc + taps[t] * pltpu.roll(src, (HALF - t) % N, 1)
                moved.append(acc)
            a_re, a_im = azf_v[0, frows, :], azf_v[1, frows, :]
            vals.append(
                (moved[0] * a_re - moved[1] * a_im, moved[0] * a_im + moved[1] * a_re)
            )
        vals = fft32(vals, 1)
        for j in range(J):
            a_re, a_im = aztw[j, 0, rows, :], aztw[j, 1, rows, :]
            v_re, v_im = vals[j]
            y_v[j, 0, rows, :] = v_re * a_re + v_im * a_im
            y_v[j, 1, rows, :] = v_im * a_re - v_re * a_im
        return c

    lax.fori_loop(0, 16, focus, 0)

    def finish(pair, c):
        data = jnp.concatenate(
            [
                jnp.concatenate([y_v[2 * pair + i, 0], y_v[2 * pair + i, 1]], axis=0)
                for i in range(2)
            ],
            axis=1,
        )
        done = left_mul(mats[2], mats[3], data) * (1.0 / (N * J))
        for i in range(2):
            for part in range(2):
                o_v[2 * pair + i, part] = done[part * N : part * N + N, i * N : i * N + N]
        for i in range(2):
            for part in range(2):
                pltpu.make_async_copy(
                    o_v.at[2 * pair + i, part], out.at[part, :, 2 * pair + i], out_sem
                ).start()
        return c

    lax.fori_loop(0, J // 2, finish, 0)
    pltpu.make_async_copy(o_v, o_v, out_sem).wait()
    for n, (first, count) in enumerate(CHUNKS):
        left_here = s_v.at[pl.ds(first, count), :, pl.ds(0, N - 1)]
        pltpu.make_async_copy(left_here, left_here, send_sem.at[n]).wait()


def shards(echoes, replica, rcmc_weights, az_filter):
    mats, twist, aztw = (jnp.asarray(t) for t in constant_tables())
    parts = len(CHUNKS)
    dma = pltpu.SemaphoreType.DMA
    out = pl.pallas_call(
        body,
        out_shape=jax.ShapeDtypeStruct((2, N, J, N), F32),
        in_specs=[pl.BlockSpec(memory_space=pl.ANY)] * 7,
        out_specs=pl.BlockSpec(memory_space=pl.ANY),
        scratch_shapes=[
            pltpu.VMEM((2, J, N * N), BF16),
            pltpu.VMEM((2, N * 16, N), F32),
            pltpu.VMEM((2, 2048), F32),
            pltpu.VMEM((2 * N, N), F32),
            pltpu.VMEM((2, N, N), F32),
            pltpu.VMEM((J, 2, N, N), F32),
            pltpu.VMEM((J, 2, N, N), F32),
            pltpu.VMEM((J, 2, N, N), F32),
            pltpu.VMEM((TAPS, N * J), F32),
            pltpu.VMEM((TAPS, N * J, N), F32),
            pltpu.VMEM((2, N * J, N), F32),
            pltpu.VMEM((2, N * J, N), BF16),
            pltpu.VMEM((4, 2 * N, 2 * N), BF16),
            pltpu.VMEM((2, N, N), F32),
            pltpu.VMEM((J, 2, N, N), F32),
            pltpu.VMEM((16, 2, 8, N), F32),
            pltpu.VMEM((16, 2, 8, N), F32),
            pltpu.VMEM((16, 2, 8, N), F32),
            pltpu.VMEM((16, 2, 8, N), F32),
            pltpu.VMEM((J, 2, N, N), F32),
            dma((8,)),
            dma((parts,)),
            dma((parts,)),
            dma((parts,)),
            dma((2,)),
            dma((2,)),
            dma(()),
        ],
        compiler_params=pltpu.CompilerParams(
            collective_id=0, has_side_effects=True, vmem_limit_bytes=60 * 2**20
        ),
        name="focus",
    )(echoes, replica, rcmc_weights, az_filter, mats, twist, aztw)
    return out.reshape(2, N * J, N)


def solution(mesh):
    return jax.shard_map(
        shards,
        mesh=mesh,
        in_specs=(
            P(None, ("chan", "segment", "shard"), None),
            P(),
            P(),
            P(None, None, ("segment", "shard")),
        ),
        out_specs=P(None, "chan", ("segment", "shard")),
        check_vma=False,
    )
```

```python
import functools
import math

import jax
import jax.numpy as jnp
import ml_dtypes
import numpy as np
from jax import lax
from jax.experimental import pallas as pl
from jax.experimental.pallas import tpu as pltpu
from jax.sharding import PartitionSpec as P

MESH = pl.DeviceIdType.MESH
F32 = jnp.float32
BF16 = jnp.bfloat16
TAPS = 8
HALF = TAPS // 2
N = 128
J = 32
CHUNKS = ((0, 4), (4, 8), (12, 8), (20, 12))


def constant_tables():
    k = np.arange(N)
    ang = 2.0 * np.pi * ((k[:, None] * k[None, :]) % N) / N
    c, s = np.cos(ang), -np.sin(ang)
    left = np.block([[c, -s], [s, c]]).astype(np.float32)
    mats = []
    for m in (left, left.T):
        hi = m.astype(ml_dtypes.bfloat16)
        lo = (m - hi.astype(np.float32)).astype(ml_dtypes.bfloat16)
        mats += [hi, lo]
    mats = np.stack(mats)
    ang = 2.0 * np.pi * (k[:, None] * k[None, :]) / (N * N)
    twist = np.stack([np.cos(ang), -np.sin(ang)]).astype(np.float32)
    j = np.arange(J)
    ang = 2.0 * np.pi * (j[:, None] * k[None, :]) / (N * J)
    az = np.stack([np.cos(ang), -np.sin(ang)], axis=1).astype(np.float32)
    az = np.ascontiguousarray(np.broadcast_to(az[..., None], (J, 2, N, N)))
    lanes = np.arange(N)
    packed = np.where(lanes % 8 < HALF, lanes % 8 - HALF, N + lanes % 8 - HALF)
    want = [lanes[None, :] + t - HALF for t in range(TAPS) if t != HALF]
    own = np.concatenate([lanes[:, None] == w for w in want], axis=1)
    edge = np.concatenate([packed[:, None] == w for w in want], axis=1)
    shift = np.stack([np.tile(own, (2, 1)), np.tile(edge, (2, 1))]).astype(ml_dtypes.bfloat16)
    return mats, twist, az, shift


def split(v):
    hi = v.astype(BF16)
    return hi, (v - hi.astype(F32)).astype(BF16)


def dot(a, b):
    return jnp.dot(a, b, preferred_element_type=F32)


def left_mul(hi, lo, data):
    d_hi, d_lo = split(data)
    return dot(hi, d_hi) + dot(lo, d_hi) + dot(hi, d_lo)


def right_mul(data, hi, lo):
    d_hi, d_lo = split(data)
    return dot(d_hi, hi) + dot(d_lo, hi) + dot(d_hi, lo)


def add(a, b):
    return (a[0] + b[0], a[1] + b[1])


def sub(a, b):
    return (a[0] - b[0], a[1] - b[1])


def turn(a, angle_num, angle_den, sign):
    q = (8 * angle_num) % (8 * angle_den)
    if q == 0:
        return a
    if q == 2 * angle_den:
        return (-a[1], a[0]) if sign > 0 else (a[1], -a[0])
    if q == 4 * angle_den:
        return (-a[0], -a[1])
    if q == 6 * angle_den:
        return (a[1], -a[0]) if sign > 0 else (-a[1], a[0])
    ang = sign * 2.0 * math.pi * angle_num / angle_den
    c, s = math.cos(ang), math.sin(ang)
    return (a[0] * c - a[1] * s, a[0] * s + a[1] * c)


def fft(xs, sign):
    n = len(xs)
    if n == 1:
        return xs
    even, odd = fft(xs[0::2], sign), fft(xs[1::2], sign)
    out = [None] * n
    for k in range(n // 2):
        t = turn(odd[k], k, n, sign)
        out[k] = add(even[k], t)
        out[k + n // 2] = sub(even[k], t)
    return out


def fft32(xs, sign):
    cols = []
    for low in range(4):
        col = fft([xs[4 * high + low] for high in range(8)], sign)
        cols.append([turn(col[k], low * k, 32, sign) for k in range(8)])
    out = [None] * 32
    for k in range(8):
        four = fft([cols[low][k] for low in range(4)], sign)
        for k0 in range(4):
            out[k + 8 * k0] = four[k0]
    return out


def body(
    echoes, replica, weights, az_filter, mats_h, twist_h, aztw_h, shift_h, out,
    e_v, u_v, rep_v, x_v, kern_v, s_v, r_v, y_v, w_t, w_b, azf_v, az_v, mats, twist, aztw, shift,
    p_r, p_l, h_l, h_r, h_c, in_sem, send_sem, recv_sem, own_sem, halo_send, halo_recv, out_sem,
):
    seg, sh = lax.axis_index("segment"), lax.axis_index("shard")
    x, y, z = sh // 16, seg * 2 + (sh // 8) % 2, sh % 8
    me = seg * 64 + sh

    def peer(i):
        px, py, pz = (x + i // 32) % 4, (y + (i // 8) % 4) % 4, (z + i % 8) % 8
        s, h = py // 2, (px * 2 + py % 2) * 8 + pz
        return s, h, s * 64 + h

    loads = [
        pltpu.make_async_copy(replica, rep_v, in_sem.at[0]),
        pltpu.make_async_copy(mats_h, mats, in_sem.at[1]),
        pltpu.make_async_copy(twist_h, twist, in_sem.at[2]),
        pltpu.make_async_copy(echoes.at[:, pl.ds(0, 16)], e_v.at[:, pl.ds(0, 16)], in_sem.at[3]),
        pltpu.make_async_copy(echoes.at[:, pl.ds(16, 16)], e_v.at[:, pl.ds(16, 16)], in_sem.at[4]),
        pltpu.make_async_copy(weights, w_t, in_sem.at[5]),
        pltpu.make_async_copy(az_filter, az_v, in_sem.at[6]),
        pltpu.make_async_copy(aztw_h, aztw, in_sem.at[7]),
        pltpu.make_async_copy(shift_h, shift, in_sem.at[8]),
    ]
    for load in loads:
        load.start()
    barrier = pltpu.get_barrier_semaphore()

    def greet(i, c):
        s, h, _ = peer(i)
        pl.semaphore_signal(
            barrier, inc=1, device_id={"segment": s, "shard": h}, device_id_type=MESH
        )
        return c

    lax.fori_loop(1, N, greet, 0)

    for i in range(3):
        loads[i].wait()
    x_v[...] = jnp.zeros_like(x_v)
    for a in range(16):
        x_v[pl.ds(a, 1), :] = rep_v[0:1, 128 * a : 128 * a + 128]
        x_v[pl.ds(128 + a, 1), :] = rep_v[1:2, 128 * a : 128 * a + 128]
    t_re, t_im = twist[0], twist[1]
    mid = left_mul(mats[0], mats[1], x_v[...])
    m_re, m_im = mid[:N], mid[N:]
    mid = jnp.concatenate([m_re * t_re - m_im * t_im, m_re * t_im + m_im * t_re], axis=1)
    spec = right_mul(mid, mats[2], mats[3]) * (1.0 / (N * N))
    kern_v[0] = spec[:, :N]
    kern_v[1] = spec[:, N:]

    def unpack(half):
        def one(a, c):
            cols = pl.ds(pl.multiple_of(a * 128, 128), 128)
            rows = pl.ds(pl.multiple_of(a * 16, 16), 16)
            for part in range(2):
                u_v[part, rows, :] = e_v[part, pl.ds(16 * half, 16), cols].astype(F32)
            return c

        lax.fori_loop(0, N, one, 0, unroll=8)

    def compress(pair, c):
        p = (2 * pair) % 16
        data = jnp.concatenate(
            [
                jnp.concatenate(
                    [u_v[part, pl.ds(p + i, N, stride=16), :] for part in range(2)], axis=0
                )
                for i in range(2)
            ],
            axis=1,
        ).astype(BF16)
        mid = dot(mats[0], data) + dot(mats[1], data)
        rows = []
        for i in range(2):
            m_re, m_im = mid[:N, i * N : i * N + N], mid[N:, i * N : i * N + N]
            rows.append(
                jnp.concatenate(
                    [m_re * twist[0] - m_im * twist[1], m_re * twist[1] + m_im * twist[0]], axis=1
                )
            )
        spec = right_mul(jnp.concatenate(rows, axis=0), mats[2], mats[3])
        rows = []
        for i in range(2):
            s_re, s_im = spec[i * N : i * N + N, :N], spec[i * N : i * N + N, N:]
            rows.append(
                jnp.concatenate(
                    [s_re * kern_v[0] + s_im * kern_v[1], s_im * kern_v[0] - s_re * kern_v[1]],
                    axis=1,
                )
            )
        mid = right_mul(jnp.concatenate(rows, axis=0), mats[0], mats[1])
        cols = []
        for i in range(2):
            m_re, m_im = mid[i * N : i * N + N, :N], mid[i * N : i * N + N, N:]
            cols.append(
                jnp.concatenate(
                    [m_re * twist[0] + m_im * twist[1], m_im * twist[0] - m_re * twist[1]], axis=0
                )
            )
        done = left_mul(mats[2], mats[3], jnp.concatenate(cols, axis=1))
        for i in range(2):
            for part in range(2):
                s_v[2 * pair + i, part] = done[part * N : part * N + N, i * N : i * N + N]
        return c

    def send(n):
        first, count = CHUNKS[n]
        rows = pl.ds(first, count)
        pltpu.make_async_copy(s_v.at[rows, :, me], r_v.at[rows, :, me], own_sem.at[n]).start()

        def one(i, c):
            s, h, at = peer(i)
            pltpu.make_async_remote_copy(
                src_ref=s_v.at[rows, :, at],
                dst_ref=r_v.at[rows, :, me],
                send_sem=send_sem.at[n],
                recv_sem=recv_sem.at[n],
                device_id={"segment": s, "shard": h},
                device_id_type=MESH,
            ).start()
            return c

        lax.fori_loop(1, N, one, 0)

    loads[3].wait()
    unpack(0)
    half = 0
    for n, (first, count) in enumerate(CHUNKS):
        start = first
        if first < 16 < first + count:
            lax.fori_loop(first // 2, 8, compress, 0)
            start = 16
        if start >= 16 and half == 0:
            half = 1
            loads[4].wait()
            unpack(1)
        lax.fori_loop(start // 2, (first + count) // 2, compress, 0)
        if n == 0:
            pl.semaphore_wait(barrier, N - 1)
        send(n)

    loads[5].wait()

    def spread(g, c):
        cols = pl.ds(pl.multiple_of(g * 128, 128), 128)
        across = jnp.transpose(w_t[:, cols])
        for t in range(TAPS):
            w_b[t, cols, :] = jnp.broadcast_to(across[:, t : t + 1], (N, N))
        return c

    lax.fori_loop(0, J, spread, 0)
    loads[6].wait()

    def widen(g, c):
        rows = pl.ds(pl.multiple_of(g * 128, 128), 128)
        for part in range(2):
            azf_v[part, rows, :] = az_v[part, rows, :].astype(F32)
        return c

    lax.fori_loop(0, J, widen, 0)
    loads[7].wait()
    loads[8].wait()

    def over_devices(pair, c):
        data = jnp.concatenate(
            [
                jnp.concatenate([r_v[2 * pair + i, 0], r_v[2 * pair + i, 1]], axis=0)
                for i in range(2)
            ],
            axis=1,
        )
        mid = left_mul(mats[0], mats[1], data)
        for i in range(2):
            m_re, m_im = mid[:N, i * N : i * N + N], mid[N:, i * N : i * N + N]
            a_re, a_im = aztw[2 * pair + i, 0], aztw[2 * pair + i, 1]
            y_v[2 * pair + i, 0] = m_re * a_re - m_im * a_im
            y_v[2 * pair + i, 1] = m_re * a_im + m_im * a_re
        return c

    for n, (first, count) in enumerate(CHUNKS):
        rows = pl.ds(first, count)
        pltpu.make_async_copy(s_v.at[rows, :, me], r_v.at[rows, :, me], own_sem.at[n]).wait()
        landed = r_v.at[rows, :, pl.ds(0, N - 1)]
        pltpu.make_async_copy(landed, landed, recv_sem.at[n]).wait()
        lax.fori_loop(first // 2, (first + count) // 2, over_devices, 0)

    lane = lax.broadcasted_iota(jnp.int32, (8, N), 1)
    slot = lane % 8

    def over_pulses(blk, c):
        rows = pl.ds(pl.multiple_of(blk * 8, 8), 8)
        vals = fft32([(y_v[j, 0, rows, :], y_v[j, 1, rows, :]) for j in range(J)], -1)
        for f2 in range(J):
            y_v[f2, 0, rows, :] = vals[f2][0]
            y_v[f2, 1, rows, :] = vals[f2][1]
        for grp in range(2):
            packed = []
            for part in range(2):
                acc = jnp.zeros((8, N), F32)
                for g in range(16):
                    moved = pltpu.roll(vals[16 * grp + g][part], (8 * g + 4) % N, 1)
                    acc = jnp.where(lane // 8 == g, moved, acc)
                packed.append(acc)
            p_r[blk, grp] = jnp.where(slot < 4, packed[0], pltpu.roll(packed[1], 4, 1))
            p_l[blk, grp] = jnp.where(slot < 4, pltpu.roll(packed[0], N - 4, 1), packed[1])
        return c

    lax.fori_loop(0, 16, over_pulses, 0)
    after, before = (me + 1) % N, (me + N - 1) % N
    right = {"segment": after // 64, "shard": after % 64}
    left = {"segment": before // 64, "shard": before % 64}
    to_right = pltpu.make_async_remote_copy(
        src_ref=p_r, dst_ref=h_l, send_sem=halo_send.at[0], recv_sem=halo_recv.at[0],
        device_id=right, device_id_type=MESH,
    )
    to_left = pltpu.make_async_remote_copy(
        src_ref=p_l, dst_ref=h_r, send_sem=halo_send.at[1], recv_sem=halo_recv.at[1],
        device_id=left, device_id_type=MESH,
    )
    to_right.start()
    to_left.start()
    to_right.wait()
    to_left.wait()

    has_left = jnp.where(me == 0, 0.0, 1.0)
    has_right = jnp.where(me == N - 1, 0.0, 1.0)

    for blk in range(16):
        for grp in range(2):
            lft = h_l[blk, grp] * has_left
            rgt = h_r[blk, grp] * has_right
            rows = slice(8 * blk, 8 * blk + 8)
            h_c[grp, 0, rows, :] = jnp.where(slot < HALF, lft, pltpu.roll(rgt, 4, 1))
            h_c[grp, 1, rows, :] = jnp.where(slot < HALF, pltpu.roll(lft, N - 4, 1), rgt)

    place = lax.broadcasted_iota(jnp.int32, (N, N), 1) // 8

    def migrate(f2, c):
        frows = pl.ds(pl.multiple_of(f2 * 128, 128), 128)
        own = jnp.concatenate([y_v[f2, 0], y_v[f2, 1]], axis=0)
        mask = place == f2 % 16
        edge = [jnp.where(mask, h_c[f2 // 16, part], 0.0) for part in range(2)]
        edge = jnp.concatenate(edge, axis=0)
        moved = dot(jnp.concatenate(split(own), axis=1), shift[0])
        moved = moved + dot(jnp.concatenate(split(edge), axis=1), shift[1])
        sums = []
        for part in range(2):
            rows = slice(part * N, part * N + N)
            acc = w_b[HALF, frows, :] * own[rows]
            for i, t in enumerate(t for t in range(TAPS) if t != HALF):
                acc = acc + w_b[t, frows, :] * moved[rows, i * N : i * N + N]
            sums.append(acc)
        a_re, a_im = azf_v[0, frows, :], azf_v[1, frows, :]
        y_v[f2, 0] = sums[0] * a_re - sums[1] * a_im
        y_v[f2, 1] = sums[0] * a_im + sums[1] * a_re
        return c

    lax.fori_loop(0, J, migrate, 0)

    def back_over_pulses(blk, c):
        rows = pl.ds(pl.multiple_of(blk * 8, 8), 8)
        vals = fft32([(y_v[f2, 0, rows, :], y_v[f2, 1, rows, :]) for f2 in range(J)], 1)
        for j in range(J):
            a_re, a_im = aztw[j, 0, rows, :], aztw[j, 1, rows, :]
            v_re, v_im = vals[j]
            y_v[j, 0, rows, :] = v_re * a_re + v_im * a_im
            y_v[j, 1, rows, :] = v_im * a_re - v_re * a_im
        pltpu.make_async_copy(y_v.at[:, :, rows], out.at[:, :, rows], out_sem).start()
        return c

    lax.fori_loop(0, 16, back_over_pulses, 0)
    pltpu.make_async_copy(y_v, out, out_sem).wait()
    for n, (first, count) in enumerate(CHUNKS):
        left_here = s_v.at[pl.ds(first, count), :, pl.ds(0, N - 1)]
        pltpu.make_async_copy(left_here, left_here, send_sem.at[n]).wait()


def finish(vals, mats_h, out, y_v, mats, o_v, in_sem, out_sem):
    loads = [pltpu.make_async_copy(mats_h.at[pl.ds(2, 2)], mats, in_sem.at[4])]
    for q in range(4):
        rows = pl.ds(8 * q, 8)
        loads.append(pltpu.make_async_copy(vals.at[rows], y_v.at[rows], in_sem.at[q]))
    for load in loads:
        load.start()
    loads[0].wait()

    def one(pair, c):
        data = jnp.concatenate(
            [
                jnp.concatenate([y_v[2 * pair + i, 0], y_v[2 * pair + i, 1]], axis=0)
                for i in range(2)
            ],
            axis=1,
        )
        done = left_mul(mats[0], mats[1], data) * (1.0 / (N * J))
        for i in range(2):
            for part in range(2):
                o_v[2 * pair + i, part] = done[part * N : part * N + N, i * N : i * N + N]
        for i in range(2):
            for part in range(2):
                pltpu.make_async_copy(
                    o_v.at[2 * pair + i, part], out.at[part, :, 2 * pair + i], out_sem
                ).start()
        return c

    for q in range(4):
        loads[q + 1].wait()
        lax.fori_loop(4 * q, 4 * q + 4, one, 0)
    pltpu.make_async_copy(o_v, o_v, out_sem).wait()


def shards(echoes, replica, rcmc_weights, az_filter):
    mats, twist, aztw, shift = (jnp.asarray(t) for t in constant_tables())
    parts = len(CHUNKS)
    dma = pltpu.SemaphoreType.DMA
    vals = pl.pallas_call(
        body,
        out_shape=jax.ShapeDtypeStruct((J, 2, N, N), F32),
        in_specs=[pl.BlockSpec(memory_space=pl.ANY)] * 8,
        out_specs=pl.BlockSpec(memory_space=pl.ANY),
        scratch_shapes=[
            pltpu.VMEM((2, J, N * N), BF16),
            pltpu.VMEM((2, N * 16, N), F32),
            pltpu.VMEM((2, 2048), F32),
            pltpu.VMEM((2 * N, N), F32),
            pltpu.VMEM((2, N, N), F32),
            pltpu.VMEM((J, 2, N, N), F32),
            pltpu.VMEM((J, 2, N, N), F32),
            pltpu.VMEM((J, 2, N, N), F32),
            pltpu.VMEM((TAPS, N * J), F32),
            pltpu.VMEM((TAPS, N * J, N), F32),
            pltpu.VMEM((2, N * J, N), F32),
            pltpu.VMEM((2, N * J, N), BF16),
            pltpu.VMEM((4, 2 * N, 2 * N), BF16),
            pltpu.VMEM((2, N, N), F32),
            pltpu.VMEM((J, 2, N, N), F32),
            pltpu.VMEM((2, 2 * N, 7 * N), BF16),
            pltpu.VMEM((16, 2, 8, N), F32),
            pltpu.VMEM((16, 2, 8, N), F32),
            pltpu.VMEM((16, 2, 8, N), F32),
            pltpu.VMEM((16, 2, 8, N), F32),
            pltpu.VMEM((2, 2, N, N), F32),
            dma((9,)),
            dma((parts,)),
            dma((parts,)),
            dma((parts,)),
            dma((2,)),
            dma((2,)),
            dma(()),
        ],
        compiler_params=pltpu.CompilerParams(
            collective_id=0, has_side_effects=True, vmem_limit_bytes=60 * 2**20
        ),
        name="focus",
    )(echoes, replica, rcmc_weights, az_filter, mats, twist, aztw, shift)
    out = pl.pallas_call(
        finish,
        out_shape=jax.ShapeDtypeStruct((2, N, J, N), F32),
        in_specs=[pl.BlockSpec(memory_space=pl.ANY)] * 2,
        out_specs=pl.BlockSpec(memory_space=pl.ANY),
        scratch_shapes=[
            pltpu.VMEM((J, 2, N, N), F32),
            pltpu.VMEM((2, 2 * N, 2 * N), BF16),
            pltpu.VMEM((J, 2, N, N), F32),
            dma((5,)),
            dma(()),
        ],
        compiler_params=pltpu.CompilerParams(vmem_limit_bytes=48 * 2**20),
        name="finish",
    )(vals, mats)
    return out.reshape(2, N * J, N)


def solution(mesh):
    return jax.shard_map(
        shards,
        mesh=mesh,
        in_specs=(
            P(None, ("chan", "segment", "shard"), None),
            P(),
            P(),
            P(None, None, ("segment", "shard")),
        ),
        out_specs=P(None, "chan", ("segment", "shard")),
        check_vma=False,
    )
```

```python
import functools
import math

import jax
import jax.numpy as jnp
import ml_dtypes
import numpy as np
from jax import lax
from jax.experimental import pallas as pl
from jax.experimental.pallas import tpu as pltpu
from jax.sharding import PartitionSpec as P

MESH = pl.DeviceIdType.MESH
F32 = jnp.float32
BF16 = jnp.bfloat16
TAPS = 8
HALF = TAPS // 2
N = 128
J = 32
CHUNKS = ((0, 4), (4, 8), (12, 12), (24, 8))


def constant_tables():
    k = np.arange(N)
    ang = 2.0 * np.pi * ((k[:, None] * k[None, :]) % N) / N
    c, s = np.cos(ang), -np.sin(ang)
    left = np.block([[c, -s], [s, c]]).astype(np.float32)
    mats = []
    for m in (left, left.T):
        hi = m.astype(ml_dtypes.bfloat16)
        lo = (m - hi.astype(np.float32)).astype(ml_dtypes.bfloat16)
        mats += [hi, lo]
    mats = np.stack(mats)
    ang = 2.0 * np.pi * (k[:, None] * k[None, :]) / (N * N)
    twist = np.stack([np.cos(ang), -np.sin(ang)]).astype(np.float32)
    j = np.arange(J)
    ang = 2.0 * np.pi * (j[:, None] * k[None, :]) / (N * J)
    az = np.stack([np.cos(ang), -np.sin(ang)], axis=1).astype(np.float32)
    az = np.ascontiguousarray(np.broadcast_to(az[..., None], (J, 2, N, N)))
    lanes = np.arange(N)
    packed = np.where(lanes % 8 < HALF, lanes % 8, N - 8 + lanes % 8)
    want = [lanes[None, :] + t - HALF for t in range(TAPS) if t != HALF]
    own = np.concatenate([lanes[:, None] == w for w in want], axis=1)
    edge = np.pad(packed[:, None] == lanes[None, :], ((0, 0), (0, 6 * N)))
    shift = np.stack([np.tile(own, (2, 1)), np.tile(edge, (2, 1))]).astype(ml_dtypes.bfloat16)
    return mats, twist, az, shift


def split(v):
    hi = v.astype(BF16)
    return hi, (v - hi.astype(F32)).astype(BF16)


def dot(a, b):
    return jnp.dot(a, b, preferred_element_type=F32)


def left_mul(hi, lo, data):
    d_hi, d_lo = split(data)
    return dot(hi, d_hi) + dot(lo, d_hi) + dot(hi, d_lo)


def right_mul(data, hi, lo):
    d_hi, d_lo = split(data)
    return dot(d_hi, hi) + dot(d_lo, hi) + dot(d_hi, lo)


def add(a, b):
    return (a[0] + b[0], a[1] + b[1])


def sub(a, b):
    return (a[0] - b[0], a[1] - b[1])


def turn(a, angle_num, angle_den, sign):
    q = (8 * angle_num) % (8 * angle_den)
    if q == 0:
        return a
    if q == 2 * angle_den:
        return (-a[1], a[0]) if sign > 0 else (a[1], -a[0])
    if q == 4 * angle_den:
        return (-a[0], -a[1])
    if q == 6 * angle_den:
        return (a[1], -a[0]) if sign > 0 else (-a[1], a[0])
    ang = sign * 2.0 * math.pi * angle_num / angle_den
    c, s = math.cos(ang), math.sin(ang)
    return (a[0] * c - a[1] * s, a[0] * s + a[1] * c)


def fft(xs, sign):
    n = len(xs)
    if n == 1:
        return xs
    even, odd = fft(xs[0::2], sign), fft(xs[1::2], sign)
    out = [None] * n
    for k in range(n // 2):
        t = turn(odd[k], k, n, sign)
        out[k] = add(even[k], t)
        out[k + n // 2] = sub(even[k], t)
    return out


def fft32(xs, sign):
    cols = []
    for low in range(4):
        col = fft([xs[4 * high + low] for high in range(8)], sign)
        cols.append([turn(col[k], low * k, 32, sign) for k in range(8)])
    out = [None] * 32
    for k in range(8):
        four = fft([cols[low][k] for low in range(4)], sign)
        for k0 in range(4):
            out[k + 8 * k0] = four[k0]
    return out


def body(
    echoes, replica, weights, az_filter, mats_h, twist_h, aztw_h, shift_h, out,
    e_v, u_v, rep_v, x_v, kern_v, s_v, r_v, y_v, w_t, w_b, azf_v, az_v, mats, twist, aztw, shift,
    p_r, p_l, h_l, h_r, h_c, w_p, in_sem, send_sem, recv_sem, own_sem, halo_send, halo_recv, out_sem,
):
    seg, sh = lax.axis_index("segment"), lax.axis_index("shard")
    x, y, z = sh // 16, seg * 2 + (sh // 8) % 2, sh % 8
    me = seg * 64 + sh

    def peer(i):
        px, py, pz = (x + i // 32) % 4, (y + (i // 8) % 4) % 4, (z + i % 8) % 8
        s, h = py // 2, (px * 2 + py % 2) * 8 + pz
        return s, h, s * 64 + h

    loads = [
        pltpu.make_async_copy(replica, rep_v, in_sem.at[0]),
        pltpu.make_async_copy(mats_h, mats, in_sem.at[1]),
        pltpu.make_async_copy(twist_h, twist, in_sem.at[2]),
        pltpu.make_async_copy(echoes.at[:, pl.ds(0, 16)], e_v.at[:, pl.ds(0, 16)], in_sem.at[3]),
        pltpu.make_async_copy(echoes.at[:, pl.ds(16, 16)], e_v.at[:, pl.ds(16, 16)], in_sem.at[4]),
        pltpu.make_async_copy(weights, w_t, in_sem.at[5]),
        pltpu.make_async_copy(az_filter, az_v, in_sem.at[6]),
        pltpu.make_async_copy(aztw_h, aztw, in_sem.at[7]),
        pltpu.make_async_copy(shift_h, shift, in_sem.at[8]),
    ]
    for load in loads:
        load.start()
    barrier = pltpu.get_barrier_semaphore()

    def greet(i, c):
        s, h, _ = peer(i)
        pl.semaphore_signal(
            barrier, inc=1, device_id={"segment": s, "shard": h}, device_id_type=MESH
        )
        return c

    lax.fori_loop(1, N, greet, 0)

    for i in range(3):
        loads[i].wait()
    x_v[...] = jnp.zeros_like(x_v)
    for a in range(16):
        x_v[pl.ds(a, 1), :] = rep_v[0:1, 128 * a : 128 * a + 128]
        x_v[pl.ds(128 + a, 1), :] = rep_v[1:2, 128 * a : 128 * a + 128]
    t_re, t_im = twist[0], twist[1]
    mid = left_mul(mats[0], mats[1], x_v[...])
    m_re, m_im = mid[:N], mid[N:]
    mid = jnp.concatenate([m_re * t_re - m_im * t_im, m_re * t_im + m_im * t_re], axis=1)
    spec = right_mul(mid, mats[2], mats[3]) * (1.0 / (N * N))
    kern_v[0] = spec[:, :N]
    kern_v[1] = spec[:, N:]

    def unpack(half):
        def one(a, c):
            cols = pl.ds(pl.multiple_of(a * 128, 128), 128)
            rows = pl.ds(pl.multiple_of(a * 16, 16), 16)
            for part in range(2):
                u_v[part, rows, :] = e_v[part, pl.ds(16 * half, 16), cols].astype(F32)
            return c

        lax.fori_loop(0, N, one, 0, unroll=8)

    def compress(pair, c):
        p = (2 * pair) % 16
        data = jnp.concatenate(
            [
                jnp.concatenate(
                    [u_v[part, pl.ds(p + i, N, stride=16), :] for part in range(2)], axis=0
                )
                for i in range(2)
            ],
            axis=1,
        ).astype(BF16)
        mid = dot(mats[0], data) + dot(mats[1], data)
        rows = []
        for i in range(2):
            m_re, m_im = mid[:N, i * N : i * N + N], mid[N:, i * N : i * N + N]
            rows.append(
                jnp.concatenate(
                    [m_re * twist[0] - m_im * twist[1], m_re * twist[1] + m_im * twist[0]], axis=1
                )
            )
        spec = right_mul(jnp.concatenate(rows, axis=0), mats[2], mats[3])
        rows = []
        for i in range(2):
            s_re, s_im = spec[i * N : i * N + N, :N], spec[i * N : i * N + N, N:]
            rows.append(
                jnp.concatenate(
                    [s_re * kern_v[0] + s_im * kern_v[1], s_im * kern_v[0] - s_re * kern_v[1]],
                    axis=1,
                )
            )
        mid = right_mul(jnp.concatenate(rows, axis=0), mats[0], mats[1])
        cols = []
        for i in range(2):
            m_re, m_im = mid[i * N : i * N + N, :N], mid[i * N : i * N + N, N:]
            cols.append(
                jnp.concatenate(
                    [m_re * twist[0] + m_im * twist[1], m_im * twist[0] - m_re * twist[1]], axis=0
                )
            )
        done = left_mul(mats[2], mats[3], jnp.concatenate(cols, axis=1))
        for i in range(2):
            for part in range(2):
                s_v[2 * pair + i, part] = done[part * N : part * N + N, i * N : i * N + N]
        return c

    def send(n):
        first, count = CHUNKS[n]
        rows = pl.ds(first, count)
        pltpu.make_async_copy(s_v.at[rows, :, me], r_v.at[rows, :, me], own_sem.at[n]).start()

        def one(i, c):
            s, h, at = peer(i)
            pltpu.make_async_remote_copy(
                src_ref=s_v.at[rows, :, at],
                dst_ref=r_v.at[rows, :, me],
                send_sem=send_sem.at[n],
                recv_sem=recv_sem.at[n],
                device_id={"segment": s, "shard": h},
                device_id_type=MESH,
            ).start()
            return c

        lax.fori_loop(1, N, one, 0)

    loads[3].wait()
    unpack(0)
    half = 0
    for n, (first, count) in enumerate(CHUNKS):
        start = first
        if first < 16 < first + count:
            lax.fori_loop(first // 2, 8, compress, 0)
            start = 16
        if start >= 16 and half == 0:
            half = 1
            loads[4].wait()
            unpack(1)
        lax.fori_loop(start // 2, (first + count) // 2, compress, 0, unroll=2 if n == 0 else 1)
        if n == 0:
            pl.semaphore_wait(barrier, N - 1)
        send(n)

    loads[5].wait()

    def spread(g, c):
        cols = pl.ds(pl.multiple_of(g * 128, 128), 128)
        across = jnp.transpose(w_t[:, cols])
        for t in range(TAPS):
            w_b[t, cols, :] = jnp.broadcast_to(across[:, t : t + 1], (N, N))
        return c

    lax.fori_loop(0, J, spread, 0)
    place = lax.broadcasted_iota(jnp.int32, (N, N), 1) // 8
    slots = lax.broadcasted_iota(jnp.int32, (N, N), 1) % 8

    def pack(i, c):
        acc = jnp.zeros((N, N), F32)
        for g in range(16):
            rows = pl.ds(pl.multiple_of((i % 2) * (16 * N) + g * N, N), N)
            acc = jnp.where(place == g, w_b[i // 2, rows, :], acc)
        w_p[i] = acc
        return c

    lax.fori_loop(0, 2 * TAPS, pack, 0)
    loads[6].wait()

    def widen(g, c):
        rows = pl.ds(pl.multiple_of(g * 128, 128), 128)
        for part in range(2):
            azf_v[part, rows, :] = az_v[part, rows, :].astype(F32)
        return c

    lax.fori_loop(0, J, widen, 0)
    loads[7].wait()
    loads[8].wait()

    def over_devices(pair, c):
        data = jnp.concatenate(
            [
                jnp.concatenate([r_v[2 * pair + i, 0], r_v[2 * pair + i, 1]], axis=0)
                for i in range(2)
            ],
            axis=1,
        )
        mid = left_mul(mats[0], mats[1], data)
        for i in range(2):
            m_re, m_im = mid[:N, i * N : i * N + N], mid[N:, i * N : i * N + N]
            a_re, a_im = aztw[2 * pair + i, 0], aztw[2 * pair + i, 1]
            y_v[2 * pair + i, 0] = m_re * a_re - m_im * a_im
            y_v[2 * pair + i, 1] = m_re * a_im + m_im * a_re
        return c

    for n, (first, count) in enumerate(CHUNKS):
        rows = pl.ds(first, count)
        pltpu.make_async_copy(s_v.at[rows, :, me], r_v.at[rows, :, me], own_sem.at[n]).wait()
        landed = r_v.at[rows, :, pl.ds(0, N - 1)]
        pltpu.make_async_copy(landed, landed, recv_sem.at[n]).wait()
        lax.fori_loop(first // 2, (first + count) // 2, over_devices, 0, unroll=2)

    lane = lax.broadcasted_iota(jnp.int32, (8, N), 1)
    slot = lane % 8

    def over_pulses(blk, c):
        rows = pl.ds(pl.multiple_of(blk * 8, 8), 8)
        vals = fft32([(y_v[j, 0, rows, :], y_v[j, 1, rows, :]) for j in range(J)], -1)
        for f2 in range(J):
            y_v[f2, 0, rows, :] = vals[f2][0]
            y_v[f2, 1, rows, :] = vals[f2][1]
        for grp in range(2):
            packed = []
            for part in range(2):
                acc = jnp.zeros((8, N), F32)
                for g in range(16):
                    moved = pltpu.roll(vals[16 * grp + g][part], (8 * g + 4) % N, 1)
                    acc = jnp.where(lane // 8 == g, moved, acc)
                packed.append(acc)
            p_r[blk, grp] = jnp.where(slot < 4, packed[0], pltpu.roll(packed[1], 4, 1))
            p_l[blk, grp] = jnp.where(slot < 4, pltpu.roll(packed[0], N - 4, 1), packed[1])
        return c

    lax.fori_loop(0, 16, over_pulses, 0)
    after, before = (me + 1) % N, (me + N - 1) % N
    right = {"segment": after // 64, "shard": after % 64}
    left = {"segment": before // 64, "shard": before % 64}
    to_right = pltpu.make_async_remote_copy(
        src_ref=p_r, dst_ref=h_l, send_sem=halo_send.at[0], recv_sem=halo_recv.at[0],
        device_id=right, device_id_type=MESH,
    )
    to_left = pltpu.make_async_remote_copy(
        src_ref=p_l, dst_ref=h_r, send_sem=halo_send.at[1], recv_sem=halo_recv.at[1],
        device_id=left, device_id_type=MESH,
    )
    to_right.start()
    to_left.start()

    def gather(f2, c):
        frows = pl.ds(pl.multiple_of(f2 * 128, 128), 128)
        own = jnp.concatenate([y_v[f2, 0], y_v[f2, 1]], axis=0)
        moved = dot(jnp.concatenate(split(own), axis=1), shift[0])
        for part in range(2):
            rows = slice(part * N, part * N + N)
            acc = w_b[HALF, frows, :] * own[rows]
            for i, t in enumerate(t for t in range(TAPS) if t != HALF):
                acc = acc + w_b[t, frows, :] * moved[rows, i * N : i * N + N]
            y_v[f2, part] = acc
        return c

    lax.fori_loop(0, J, gather, 0, unroll=2)
    to_right.wait()
    to_left.wait()

    has_left = jnp.where(me == 0, 0.0, 1.0)
    has_right = jnp.where(me == N - 1, 0.0, 1.0)

    for blk in range(16):
        for grp in range(2):
            lft = h_l[blk, grp] * has_left
            rgt = h_r[blk, grp] * has_right
            rows = slice(8 * blk, 8 * blk + 8)
            h_c[grp, 0, rows, :] = jnp.where(slot < HALF, lft, pltpu.roll(rgt, 4, 1))
            h_c[grp, 1, rows, :] = jnp.where(slot < HALF, pltpu.roll(lft, N - 4, 1), rgt)

    for grp in range(2):
        for part in range(2):
            held = h_c[grp, part]
            acc = jnp.where(slots < HALF, w_p[grp] * held, 0.0)
            for t in range(1, TAPS):
                if t != HALF:
                    moved = pltpu.roll(held, N - t if t < HALF else TAPS - t, 1)
                    used = slots < HALF - t if t < HALF else slots >= TAPS + HALF - t
                    acc = acc + jnp.where(used, w_p[2 * t + grp] * moved, 0.0)
            h_c[grp, part] = acc

    def migrate(f2, c):
        frows = pl.ds(pl.multiple_of(f2 * 128, 128), 128)
        mask = place == f2 % 16
        edge = [jnp.where(mask, h_c[f2 // 16, part], 0.0) for part in range(2)]
        edge = jnp.concatenate(edge, axis=0)
        moved = dot(jnp.concatenate(split(edge), axis=1), shift[1, :, :N])
        sums = [y_v[f2, part] + moved[part * N : part * N + N] for part in range(2)]
        a_re, a_im = azf_v[0, frows, :], azf_v[1, frows, :]
        y_v[f2, 0] = sums[0] * a_re - sums[1] * a_im
        y_v[f2, 1] = sums[0] * a_im + sums[1] * a_re
        return c

    lax.fori_loop(0, J, migrate, 0, unroll=4)

    def back_over_pulses(blk, c):
        rows = pl.ds(pl.multiple_of(blk * 8, 8), 8)
        vals = fft32([(y_v[f2, 0, rows, :], y_v[f2, 1, rows, :]) for f2 in range(J)], 1)
        for j in range(J):
            a_re, a_im = aztw[j, 0, rows, :], aztw[j, 1, rows, :]
            v_re, v_im = vals[j]
            y_v[j, 0, rows, :] = v_re * a_re + v_im * a_im
            y_v[j, 1, rows, :] = v_im * a_re - v_re * a_im
        pltpu.make_async_copy(y_v.at[:, :, rows], out.at[:, :, rows], out_sem).start()
        return c

    lax.fori_loop(0, 16, back_over_pulses, 0)
    pltpu.make_async_copy(y_v, out, out_sem).wait()
    for n, (first, count) in enumerate(CHUNKS):
        left_here = s_v.at[pl.ds(first, count), :, pl.ds(0, N - 1)]
        pltpu.make_async_copy(left_here, left_here, send_sem.at[n]).wait()


def finish(vals, mats_h, out, y_v, mats, o_v, in_sem, out_sem):
    loads = [pltpu.make_async_copy(mats_h.at[pl.ds(2, 2)], mats, in_sem.at[4])]
    for q in range(4):
        rows = pl.ds(8 * q, 8)
        loads.append(pltpu.make_async_copy(vals.at[rows], y_v.at[rows], in_sem.at[q]))
    for load in loads:
        load.start()
    loads[0].wait()

    def one(pair, c):
        data = jnp.concatenate(
            [
                jnp.concatenate([y_v[2 * pair + i, 0], y_v[2 * pair + i, 1]], axis=0)
                for i in range(2)
            ],
            axis=1,
        )
        done = left_mul(mats[0], mats[1], data) * (1.0 / (N * J))
        for i in range(2):
            for part in range(2):
                o_v[2 * pair + i, part] = done[part * N : part * N + N, i * N : i * N + N]
        for i in range(2):
            for part in range(2):
                pltpu.make_async_copy(
                    o_v.at[2 * pair + i, part], out.at[part, :, 2 * pair + i], out_sem
                ).start()
        return c

    for q in range(4):
        loads[q + 1].wait()
        lax.fori_loop(4 * q, 4 * q + 4, one, 0, unroll=2)
    pltpu.make_async_copy(o_v, o_v, out_sem).wait()


def shards(echoes, replica, rcmc_weights, az_filter):
    mats, twist, aztw, shift = (jnp.asarray(t) for t in constant_tables())
    parts = len(CHUNKS)
    dma = pltpu.SemaphoreType.DMA
    vals = pl.pallas_call(
        body,
        out_shape=jax.ShapeDtypeStruct((J, 2, N, N), F32),
        in_specs=[pl.BlockSpec(memory_space=pl.ANY)] * 8,
        out_specs=pl.BlockSpec(memory_space=pl.ANY),
        scratch_shapes=[
            pltpu.VMEM((2, J, N * N), BF16),
            pltpu.VMEM((2, N * 16, N), F32),
            pltpu.VMEM((2, 2048), F32),
            pltpu.VMEM((2 * N, N), F32),
            pltpu.VMEM((2, N, N), F32),
            pltpu.VMEM((J, 2, N, N), F32),
            pltpu.VMEM((J, 2, N, N), F32),
            pltpu.VMEM((J, 2, N, N), F32),
            pltpu.VMEM((TAPS, N * J), F32),
            pltpu.VMEM((TAPS, N * J, N), F32),
            pltpu.VMEM((2, N * J, N), F32),
            pltpu.VMEM((2, N * J, N), BF16),
            pltpu.VMEM((4, 2 * N, 2 * N), BF16),
            pltpu.VMEM((2, N, N), F32),
            pltpu.VMEM((J, 2, N, N), F32),
            pltpu.VMEM((2, 2 * N, 7 * N), BF16),
            pltpu.VMEM((16, 2, 8, N), F32),
            pltpu.VMEM((16, 2, 8, N), F32),
            pltpu.VMEM((16, 2, 8, N), F32),
            pltpu.VMEM((16, 2, 8, N), F32),
            pltpu.VMEM((2, 2, N, N), F32),
            pltpu.VMEM((2 * TAPS, N, N), F32),
            dma((9,)),
            dma((parts,)),
            dma((parts,)),
            dma((parts,)),
            dma((2,)),
            dma((2,)),
            dma(()),
        ],
        compiler_params=pltpu.CompilerParams(
            collective_id=0, has_side_effects=True, vmem_limit_bytes=60 * 2**20
        ),
        name="focus",
    )(echoes, replica, rcmc_weights, az_filter, mats, twist, aztw, shift)
    out = pl.pallas_call(
        finish,
        out_shape=jax.ShapeDtypeStruct((2, N, J, N), F32),
        in_specs=[pl.BlockSpec(memory_space=pl.ANY)] * 2,
        out_specs=pl.BlockSpec(memory_space=pl.ANY),
        scratch_shapes=[
            pltpu.VMEM((J, 2, N, N), F32),
            pltpu.VMEM((2, 2 * N, 2 * N), BF16),
            pltpu.VMEM((J, 2, N, N), F32),
            dma((5,)),
            dma(()),
        ],
        compiler_params=pltpu.CompilerParams(vmem_limit_bytes=60 * 2**20),
        name="finish",
    )(vals, mats)
    return out.reshape(2, N * J, N)


def solution(mesh):
    return jax.shard_map(
        shards,
        mesh=mesh,
        in_specs=(
            P(None, ("chan", "segment", "shard"), None),
            P(),
            P(),
            P(None, None, ("segment", "shard")),
        ),
        out_specs=P(None, "chan", ("segment", "shard")),
        check_vma=False,
    )
```
